32 devices in a mesh: groups: 2 (over x), blk: 16 (over z, y, core).
Axes of the slice: x: 2, y: 2, z: 4, core: 2. Of those that a mesh axis runs over, the one named last changes fastest.
Arguments:
- vertices: float32 [3, 16384], P(None, ('groups', 'blk')), parts along dimension 1, may hold values from 0 to 1
- source_tri: int32 [3, 32768], P(None, ('groups', 'blk')), parts along dimension 1, may hold values from 0 to 511
- source_disp: float32 [3, 32768], P(None, ('groups', 'blk')), parts along dimension 1, may hold values from -6 to 6
- target_tri: int32 [3, 16384], P(None, ('groups', 'blk')), parts along dimension 1, may hold values from 0 to 511
- fracture_of: int32 [16384], P(('groups', 'blk')), parts along dimension 0, may hold values from 0 to 127
- pressure_coeffs: float32 [4, 256], P(None, ('groups', 'blk')), parts along dimension 1, may hold values from -2 to 2
Outputs:
- force: float32 [3, 16384], P(None, ('groups', 'blk')), parts along dimension 1
The draws below stay inside these ranges and needn't reach their ends.
There are 2 independent parts, one for each index of `groups`. The reference program is written for one: setup_inputs(seed, part) draws one part's arguments, and reference() takes and returns one part's arrays. A program takes and returns all parts, laid end to end along the dimension named above; each array names one. Nothing has to cross between parts.
Inputs may be any that keep to these rules, and one draw needn't show every extreme that they name: `source_tri`: source triangle c uses vertices (c // 1024) * 512 + value. `target_tri`: target triangle c uses vertices (c // 512) * 512 + value.
All inputs are finite; a program needn't handle non-finite values.
Results may differ from the reference program's by a relative error of at most 0.00023.
Values sent between devices are 32-bit elements; how exact they have to be, the bound alone decides.
A program may use at most 64 MiB of HBM per device.

```python
import math
import jax
import jax.numpy as jnp
from jax import lax

TGT_DEV = 512
SRC_DEV = 1024
VERT_DEV = 512
TARGETS = 8192
SOURCES = 16384
VERTS = 8192
FRACS = 128
N_BLK = 16


def plant(drawn, own_key, low, high):
    longest = drawn.shape.index(max(drawn.shape))
    spots = []
    for shift in (0, 1):
        where = [jax.random.randint(jax.random.fold_in(own_key, axis), (), 0, length) for axis, length in enumerate(drawn.shape)]
        where[longest] = (where[longest] + shift) % drawn.shape[longest]
        spots.append(tuple(where))
    return drawn.at[spots[0]].set(low).at[spots[1]].set(high)


def level_of(stream_key, shape, cuts, low, largest):
    factor_of = 1.0
    for dim, parts in cuts:
        draws = jax.random.uniform(jax.random.fold_in(jax.random.fold_in(stream_key, 6), dim), (parts,), jnp.float32, low / len(cuts), largest / len(cuts))
        factor_of = factor_of * jnp.repeat(jnp.exp(draws), shape[dim] // parts).reshape((-1,) + (1,) * (len(shape) - 1 - dim))
    return factor_of


def bell_draw(key, extent, spread, bound, cuts=(), held_as=jnp.bfloat16):
    values = jax.random.normal(key, extent, jnp.float32) * spread
    if len(cuts) > 0:
        values = level_of(key, extent, cuts, -0.22, 0.18) * values
    return jnp.clip(values, min=-bound, max=bound).astype(held_as)


def setup_inputs(seed: int = 0, part: int = 0) -> dict:
    splits = jax.random.split(jax.random.key(seed), 7)
    part_splits = jax.random.split(jax.random.fold_in(splits[6], part), 7)
    return {
        "vertices": jnp.clip(1.0 * jax.random.uniform(part_splits[0], (3, VERTS), jnp.float32) ** level_of(part_splits[0], (3, VERTS), ((1, 16),), -0.2, 0.2), 0.0, 1.0),
        "source_tri": plant(jax.random.randint(part_splits[1], (3, SOURCES), 0, VERT_DEV), jax.random.fold_in(part_splits[1], 1), 0, VERT_DEV - 1).astype(jnp.int32),
        "source_disp": bell_draw(part_splits[2], (3, SOURCES), 1.0, 6.0, ((1, 16),), jnp.float32),
        "target_tri": plant(jax.random.randint(part_splits[3], (3, TARGETS), 0, VERT_DEV), jax.random.fold_in(part_splits[3], 1), 0, VERT_DEV - 1).astype(jnp.int32),
        "fracture_of": plant(jax.random.randint(part_splits[4], (TARGETS,), 0, FRACS), jax.random.fold_in(part_splits[4], 1), 0, FRACS - 1).astype(jnp.int32),
        "pressure_coeffs": jnp.clip(jax.random.uniform(part_splits[5], (4, FRACS), jnp.float32, -2.0, 2.0) * level_of(part_splits[5], (4, FRACS), ((1, 16),), -0.4, 0.0), -2.0, 2.0),
    }


core_sq = 0.01
force_gain = 40.0

def corners(vertices, triangles, per_block):
    tri_count = triangles.shape[1]
    base_index = jnp.arange(tri_count, dtype=jnp.int32) // per_block * VERT_DEV
    global_index = (triangles + base_index[None, :]).astype(jnp.int32)
    first = jnp.take(vertices, global_index[0], axis=1)
    second = jnp.take(vertices, global_index[1], axis=1)
    third = jnp.take(vertices, global_index[2], axis=1)
    centers = (first + second + third) / 3.0
    areas = 0.5 * jnp.cross(second - first, third - first, axis=0)
    return (centers, areas)

def pair_forces(points, normals, sources_part):
    centers = sources_part[0:3]
    areas = sources_part[3:6]
    jumps = sources_part[6:9]
    seps = [points[k][:, None] - centers[k][None, :] for k in range(3)]
    dist_sq = seps[0] * seps[0] + seps[1] * seps[1] + seps[2] * seps[2] + core_sq
    inv_dist = lax.rsqrt(dist_sq)
    normal_area = sum((normals[k][:, None] * areas[k][None, :] for k in range(3)))
    sep_jump = sum((seps[k] * jumps[k][None, :] for k in range(3)))
    normal_sep = sum((normals[k][:, None] * seps[k] for k in range(3)))
    coef_one = inv_dist * normal_area
    coef_two = inv_dist * inv_dist * inv_dist * sep_jump * normal_sep
    dims = (((1,), (1,)), ((), ()))
    part_one = lax.dot_general(jumps, coef_one, dims, precision=lax.Precision.HIGHEST)
    part_two = lax.dot_general(areas, coef_two, dims, precision=lax.Precision.HIGHEST)
    return part_one + part_two

def reference(vertices, source_tri, source_disp, target_tri, fracture_of, pressure_coeffs):
    src_centers, src_areas = corners(vertices, source_tri, SRC_DEV)
    tgt_centers, tgt_normals = corners(vertices, target_tri, TGT_DEV)
    sources = jnp.concatenate([src_centers, src_areas, source_disp], axis=0)
    src_blocks = sources.reshape(9, N_BLK, SRC_DEV).transpose(1, 0, 2)
    targets = jnp.concatenate([tgt_centers, tgt_normals], axis=0)
    tgt_blocks = targets.reshape(6, N_BLK, TGT_DEV).transpose(1, 0, 2)

    def one_target(tgt_block):

        def add_block(running, src_block):
            return (running + pair_forces(tgt_block[0:3], tgt_block[3:6], src_block), None)
        start_acc = jnp.zeros((3, TGT_DEV), jnp.float32)
        result, _ = lax.scan(add_block, start_acc, src_blocks)
        return result
    influence = lax.map(one_target, tgt_blocks).transpose(1, 0, 2).reshape(3, TARGETS)
    picked = pressure_coeffs[:, fracture_of]
    pressure = picked[0] + picked[1] * tgt_centers[0] + picked[2] * tgt_centers[1] + picked[3] * tgt_centers[2]
    gain = force_gain / math.sqrt(SOURCES)
    return gain * influence - pressure[None, :] * tgt_normals
```

```python
import functools
import math

import jax
import jax.numpy as jnp
from jax import lax
from jax.experimental import pallas as pl
from jax.experimental.pallas import tpu as pltpu
from jax.sharding import PartitionSpec as P

core_sq = 0.01
force_gain = 40.0
LANES = 128
PIECES = 3
GROUP = 2
f32 = jnp.float32
bf16 = jnp.bfloat16


def split(value, pieces):
    out = []
    for _ in range(pieces):
        piece = value.astype(bf16).astype(f32)
        out.append(piece)
        value = value - piece
    return out


def lookup(table, index):
    columns = []
    for t in range(index.shape[1] // LANES):
        where = index[:, t * LANES : (t + 1) * LANES]
        low, high = where % LANES, where // LANES
        got = None
        for c in range(table.shape[1] // LANES):
            part = jnp.broadcast_to(table[:, c * LANES : (c + 1) * LANES], (8, LANES))
            part = jnp.take_along_axis(part, low, axis=1, mode="promise_in_bounds")
            got = part if got is None else jnp.where(high == c, part, got)
        columns.append(got)
    return jnp.concatenate(columns, axis=1)


def triangles(corner, first):
    p0, p1, p2 = ([corner[k][first + c : first + c + 1] for k in range(3)] for c in range(3))
    centers = [(p0[k] + p1[k] + p2[k]) / 3.0 for k in range(3)]
    u = [p1[k] - p0[k] for k in range(3)]
    v = [p2[k] - p0[k] for k in range(3)]
    areas = [0.5 * (u[(k + 1) % 3] * v[(k + 2) % 3] - u[(k + 2) % 3] * v[(k + 1) % 3]) for k in range(3)]
    return centers, areas


def source_features(block, width):
    main = block[:, :width]
    row = lax.broadcasted_iota(jnp.int32, (8, width), 0)
    y = [main[k : k + 1] for k in range(3)]
    a = [main[3 + k : 4 + k] for k in range(3)]
    d = [main[6:7], main[7:8]]
    d.append(
        jnp.concatenate([block[t : t + 1, width : width + LANES] for t in range(width // LANES)], axis=1)
    )
    m1, m2, m3 = split(main, 3)
    q1, q2, q3 = split(main * main, 3)
    ones = jnp.ones((8, width), f32)
    near = jnp.concatenate([m1, m1, m1, m2, m2, m3, q1, q2, q3, ones], axis=0).astype(bf16)
    outer = lambda t: jnp.where(row < 3, t[0], jnp.where(row < 6, t[1], t[2]))
    inner = lambda t: jnp.where(row % 3 == 0, t[0], jnp.where(row % 3 == 1, t[1], t[2]))
    yy = y[0] * y[0] + y[1] * y[1] + y[2] * y[2] + core_sq
    yd = y[0] * d[0] + y[1] * d[1] + y[2] * d[2]
    q = outer(a) * inner(d)
    last = a[2] * d[2]
    last_c = yy * last + y[2] * yd * a[2]
    tiles = [q, y[0] * q, y[1] * q, y[2] * q, yy * q + (yd * outer(y)) * inner(a)]
    tail = jnp.where(row == 0, last, 0.0)
    for k in range(3):
        tail = jnp.where(row == k + 1, y[k] * last, tail)
    tail = jnp.where(row == 4, last_c, tail)
    weights = split(jnp.concatenate(tiles + [tail], axis=0), PIECES)
    return near, jnp.concatenate(weights, axis=0).astype(bf16)


def target_features(x):
    width = x[0].shape[1]
    row = lax.broadcasted_iota(jnp.int32, (8, width), 0)
    coords = jnp.where(row == 0, x[0], jnp.where(row == 1, x[1], jnp.where(row == 2, x[2], 0.0)))
    x1, x2, x3 = split(-2.0 * coords, 3)
    square = x[0] * x[0] + x[1] * x[1] + x[2] * x[2] + core_sq
    s1, s2, s3 = split(square, 3)
    const = jnp.where(row == 0, s1, jnp.where(row == 1, s2, jnp.where(row == 2, s3, 0.0)))
    first3 = jnp.where(row < 3, 1.0, 0.0)
    return jnp.concatenate([x1, x2, x3, x1, x2, x1, first3, first3, first3, const], axis=0).astype(bf16)


def combine(sums, x, n):
    def pick(tile, k, m):
        r = 3 * k + m
        at = 8 * tile + r if r < 8 else 40 + tile
        return sums[at : at + 1]

    first = [[pick(0, k, m) for m in range(3)] for k in range(3)]
    moved = [[[pick(1 + p, k, m) for m in range(3)] for k in range(3)] for p in range(3)]
    const = [[pick(4, k, m) for m in range(3)] for k in range(3)]
    xx = x[0] * x[0] + x[1] * x[1] + x[2] * x[2]
    nx = n[0] * x[0] + n[1] * x[1] + n[2] * x[2]
    rows = []
    for m in range(3):
        total = 0.0
        for k in range(3):
            inside = xx * first[k][m] + const[k][m]
            for p in range(3):
                inside = inside - x[p] * (2.0 * moved[p][k][m] + moved[k][m][p])
            total = total + n[k] * inside
            total = total + nx * (x[k] * first[m][k] - moved[k][m][k])
        rows.append(total)
    return rows


def kernel(
    n_dev, vert_ref, stri_ref, disp_ref, ttri_ref, frac_ref, coef_ref, out_ref,
    held, index, coef, near_t, sums, send_sem, recv_sem,
):
    me = lax.axis_index("blk")
    width = stri_ref.shape[1]
    targets = ttri_ref.shape[1]
    per_dev = coef_ref.shape[1]
    chips = n_dev // 2

    def partner(step, sign):
        chip = lax.rem(me // 2 + sign * (step // 2) + chips, chips)
        return chip * 2 + lax.rem(me + step, 2)

    barrier = pltpu.get_barrier_semaphore()

    def greet(step, _):
        pl.semaphore_signal(
            barrier, inc=1, device_id={"blk": partner(step, 1)}, device_id_type=pl.DeviceIdType.MESH
        )
        return 0

    lax.fori_loop(1, n_dev, greet, 0)

    index[...] = jnp.zeros_like(index)
    index[0:3, :] = stri_ref[...]
    index[3:6, 0:targets] = ttri_ref[...]
    spots = index[...]
    corner = [lookup(vert_ref[k : k + 1, :], spots) for k in range(3)]
    centers, areas = triangles(corner, 0)
    row = lax.broadcasted_iota(jnp.int32, (8, width), 0)
    main = disp_ref[1:2, :]
    for r, value in enumerate([c - 0.5 for c in centers] + areas + [disp_ref[0:1, :]]):
        main = jnp.where(row == r, value, main)
    lane = lax.broadcasted_iota(jnp.int32, (8, LANES), 1)
    coef[...] = jnp.zeros_like(coef)
    coef[0:4, 0:per_dev] = coef_ref[...]
    spread = jnp.take_along_axis(coef[...], lane % per_dev, axis=1, mode="promise_in_bounds")
    per_tile = LANES // per_dev
    spread = jnp.where(lane // per_dev == lax.rem(me, per_tile), spread, 0.0)
    held[me, :, 0:width] = main
    for t in range(width // LANES):
        held[me, t : t + 1, width : width + LANES] = disp_ref[2:3, t * LANES : (t + 1) * LANES]
    held[me, :, width + LANES : width + 2 * LANES] = spread

    def copy(step):
        return pltpu.make_async_remote_copy(
            src_ref=held.at[me],
            dst_ref=held.at[me],
            send_sem=send_sem.at[step],
            recv_sem=recv_sem.at[me],
            device_id={"blk": partner(step, 1)},
            device_id_type=pl.DeviceIdType.MESH,
        )

    def arrived(step):
        source = partner(step, -1)
        pltpu.make_async_remote_copy(
            src_ref=held.at[source],
            dst_ref=held.at[source],
            send_sem=send_sem.at[step],
            recv_sem=recv_sem.at[source],
            device_id={"blk": source},
            device_id_type=pl.DeviceIdType.MESH,
        ).wait_recv()
        return source

    pl.semaphore_wait(barrier, n_dev - 1)

    def send(step, _):
        copy(step).start()
        return 0

    lax.fori_loop(1, n_dev, send, 0)

    corner = [c[:, 0:targets] for c in corner]
    points, normals = triangles(corner, 3)
    x = [p - 0.5 for p in points]
    near_t[...] = target_features(x)
    sums[...] = jnp.zeros_like(sums)

    def add_blocks(sources):
        left, right = [], []
        for source in sources:
            near, weights = source_features(held[source], width)
            dist_sq = lax.dot_general(
                near, near_t[...], (((0,), (0,)), ((), ())), preferred_element_type=f32
            )
            inv = lax.rsqrt(dist_sq)
            cube = inv * inv * inv
            high = cube.astype(bf16)
            low = (cube - high.astype(f32)).astype(bf16)
            left += [weights, weights]
            right += [high, low]
        sums[...] += jnp.dot(
            jnp.concatenate(left, axis=1), jnp.concatenate(right, axis=0), preferred_element_type=f32
        )

    arrived(1)
    add_blocks([me, partner(1, -1)])

    def step_blocks(step, _):
        add_blocks([arrived(GROUP * step + g) for g in range(GROUP)])
        return 0

    lax.fori_loop(1, n_dev // GROUP, step_blocks, 0)

    total = sums[0:48, :]
    for piece in range(1, PIECES):
        total = total + sums[48 * piece : 48 * piece + 48, :]
    influence = combine(total, x, normals)

    tables = -(-n_dev * per_dev // LANES)
    which = jnp.broadcast_to(frac_ref[...], (8, targets))
    low, high = which % LANES, which // LANES
    picked = jnp.zeros((8, targets), f32)
    for g in range(tables):
        table = jnp.zeros((8, LANES), f32)
        for s in range(g * per_tile, min((g + 1) * per_tile, n_dev)):
            table = table + held[s, :, width + LANES : width + 2 * LANES]
        got = jnp.concatenate(
            [
                jnp.take_along_axis(
                    table, low[:, t * LANES : (t + 1) * LANES], axis=1, mode="promise_in_bounds"
                )
                for t in range(targets // LANES)
            ],
            axis=1,
        )
        picked = jnp.where(high == g, got, picked)
    pressure = picked[0:1]
    for k in range(3):
        pressure = pressure + picked[k + 1 : k + 2] * points[k]
    gain = force_gain / math.sqrt(width * n_dev)
    for m in range(3):
        out_ref[m : m + 1, :] = gain * influence[m] - pressure * normals[m]

    def sent(step, _):
        copy(step).wait_send()
        return 0

    lax.fori_loop(1, n_dev, sent, 0)


def solution(mesh):
    n_dev = mesh.shape["blk"]

    def local(vertices, source_tri, source_disp, target_tri, fracture_of, pressure_coeffs):
        width, targets = source_tri.shape[1], target_tri.shape[1]
        vmem = pl.BlockSpec(memory_space=pltpu.VMEM)
        return pl.pallas_call(
            functools.partial(kernel, n_dev),
            out_shape=jax.ShapeDtypeStruct((3, targets), f32),
            in_specs=[vmem] * 6,
            out_specs=vmem,
            scratch_shapes=[
                pltpu.VMEM((n_dev, 8, width + 2 * LANES), f32),
                pltpu.VMEM((8, width), jnp.int32),
                pltpu.VMEM((8, LANES), f32),
                pltpu.VMEM((80, targets), bf16),
                pltpu.VMEM((48 * PIECES, targets), f32),
                pltpu.SemaphoreType.DMA((n_dev,)),
                pltpu.SemaphoreType.DMA((n_dev,)),
            ],
            compiler_params=pltpu.CompilerParams(
                collective_id=0, has_side_effects=True, vmem_limit_bytes=48 << 20
            ),
        )(vertices, source_tri, source_disp, target_tri, fracture_of[None, :], pressure_coeffs)

    both = ("groups", "blk")
    wide = P(None, both)
    return jax.shard_map(
        local, mesh=mesh, in_specs=(wide, wide, wide, wide, P(both), wide), out_specs=wide, check_vma=False
    )
```

```python
import functools
import math

import jax
import jax.numpy as jnp
from jax import lax
from jax.experimental import pallas as pl
from jax.experimental.pallas import tpu as pltpu
from jax.sharding import PartitionSpec as P

core_sq = 0.01
force_gain = 40.0
LANES = 128
PIECES = 3
f32 = jnp.float32
bf16 = jnp.bfloat16


def split(value, pieces):
    out = []
    for _ in range(pieces):
        piece = value.astype(bf16).astype(f32)
        out.append(piece)
        value = value - piece
    return out


def lookup(table, index):
    columns = []
    for t in range(index.shape[1] // LANES):
        where = index[:, t * LANES : (t + 1) * LANES]
        low, high = where % LANES, where // LANES
        got = None
        for c in range(table.shape[1] // LANES):
            part = jnp.broadcast_to(table[:, c * LANES : (c + 1) * LANES], (8, LANES))
            part = jnp.take_along_axis(part, low, axis=1, mode="promise_in_bounds")
            got = part if got is None else jnp.where(high == c, part, got)
        columns.append(got)
    return jnp.concatenate(columns, axis=1)


def triangles(corner, first):
    p0, p1, p2 = ([corner[k][first + c : first + c + 1] for k in range(3)] for c in range(3))
    centers = [(p0[k] + p1[k] + p2[k]) / 3.0 for k in range(3)]
    u = [p1[k] - p0[k] for k in range(3)]
    v = [p2[k] - p0[k] for k in range(3)]
    areas = [0.5 * (u[(k + 1) % 3] * v[(k + 2) % 3] - u[(k + 2) % 3] * v[(k + 1) % 3]) for k in range(3)]
    return centers, areas


def source_features(block, width):
    main = block[:, :width]
    row = lax.broadcasted_iota(jnp.int32, (8, width), 0)
    y = [main[k : k + 1] for k in range(3)]
    a = [main[3 + k : 4 + k] for k in range(3)]
    d = [main[6:7], main[7:8]]
    d.append(
        jnp.concatenate([block[t : t + 1, width : width + LANES] for t in range(width // LANES)], axis=1)
    )
    m1, m2, m3 = split(main, 3)
    q1, q2, q3 = split(main * main, 3)
    ones = jnp.ones((8, width), f32)
    near = jnp.concatenate([m1, m1, m1, m2, m2, m3, q1, q2, q3, ones], axis=0).astype(bf16)
    outer = lambda t: jnp.where(row < 3, t[0], jnp.where(row < 6, t[1], t[2]))
    inner = lambda t: jnp.where(row % 3 == 0, t[0], jnp.where(row % 3 == 1, t[1], t[2]))
    yy = y[0] * y[0] + y[1] * y[1] + y[2] * y[2] + core_sq
    yd = y[0] * d[0] + y[1] * d[1] + y[2] * d[2]
    q = outer(a) * inner(d)
    last = a[2] * d[2]
    last_c = yy * last + y[2] * yd * a[2]
    tiles = [q, y[0] * q, y[1] * q, y[2] * q, yy * q + (yd * outer(y)) * inner(a)]
    tail = jnp.where(row == 0, last, 0.0)
    for k in range(3):
        tail = jnp.where(row == k + 1, y[k] * last, tail)
    tail = jnp.where(row == 4, last_c, tail)
    weights = split(jnp.concatenate(tiles + [tail], axis=0), PIECES)
    return near, jnp.concatenate(weights, axis=0).astype(bf16)


def target_features(x):
    width = x[0].shape[1]
    row = lax.broadcasted_iota(jnp.int32, (8, width), 0)
    coords = jnp.where(row == 0, x[0], jnp.where(row == 1, x[1], jnp.where(row == 2, x[2], 0.0)))
    x1, x2, x3 = split(-2.0 * coords, 3)
    square = x[0] * x[0] + x[1] * x[1] + x[2] * x[2] + core_sq
    s1, s2, s3 = split(square, 3)
    const = jnp.where(row == 0, s1, jnp.where(row == 1, s2, jnp.where(row == 2, s3, 0.0)))
    first3 = jnp.where(row < 3, 1.0, 0.0)
    return jnp.concatenate([x1, x2, x3, x1, x2, x1, first3, first3, first3, const], axis=0).astype(bf16)


def combine(sums, x, n):
    def pick(tile, k, m):
        r = 3 * k + m
        at = 8 * tile + r if r < 8 else 40 + tile
        return sums[at : at + 1]

    first = [[pick(0, k, m) for m in range(3)] for k in range(3)]
    moved = [[[pick(1 + p, k, m) for m in range(3)] for k in range(3)] for p in range(3)]
    const = [[pick(4, k, m) for m in range(3)] for k in range(3)]
    xx = x[0] * x[0] + x[1] * x[1] + x[2] * x[2]
    nx = n[0] * x[0] + n[1] * x[1] + n[2] * x[2]
    rows = []
    for m in range(3):
        total = 0.0
        for k in range(3):
            inside = xx * first[k][m] + const[k][m]
            for p in range(3):
                inside = inside - x[p] * (2.0 * moved[p][k][m] + moved[k][m][p])
            total = total + n[k] * inside
            total = total + nx * (x[k] * first[m][k] - moved[k][m][k])
        rows.append(total)
    return rows


def kernel(
    n_dev, vert_ref, stri_ref, disp_ref, ttri_ref, frac_ref, coef_ref, out_ref,
    held, index, coef, near_t, sums, send_sem, recv_sem,
):
    me = lax.axis_index("blk")
    width = stri_ref.shape[1]
    targets = ttri_ref.shape[1]
    per_dev = coef_ref.shape[1]
    chips = n_dev // 2
    inner = 1 << (chips.bit_length() - 1) // 2
    outer = chips // inner
    core = lax.rem(me, 2)
    sibling = me + 1 - 2 * core
    row_at = lax.rem(me // 2, inner)
    column_at = me // (2 * inner)

    def block_of(step):
        o = lax.rem(column_at - lax.rem(step, outer) + outer, outer)
        i = lax.rem(row_at - step // outer + inner, inner)
        return (o * inner + i) * 2 + core

    def outer_peer(step):
        return (lax.rem(column_at + step, outer) * inner + row_at) * 2 + core

    def inner_peer(step):
        return (column_at * inner + lax.rem(row_at + step, inner)) * 2 + core

    barrier = pltpu.get_barrier_semaphore()

    def greet(device):
        pl.semaphore_signal(
            barrier, inc=1, device_id={"blk": device}, device_id_type=pl.DeviceIdType.MESH
        )

    def each(low, high, act):
        def body(step, _):
            act(step)
            return 0

        lax.fori_loop(low, high, body, 0)

    greet(sibling)
    each(1, outer, lambda j: greet(outer_peer(j)))
    each(1, inner, lambda j: greet(inner_peer(j)))

    index[...] = jnp.zeros_like(index)
    index[0:3, :] = stri_ref[...]
    index[3:6, 0:targets] = ttri_ref[...]
    spots = index[...]
    corner = [lookup(vert_ref[k : k + 1, :], spots) for k in range(3)]
    centers, areas = triangles(corner, 0)
    row = lax.broadcasted_iota(jnp.int32, (8, width), 0)
    main = disp_ref[1:2, :]
    for r, value in enumerate([c - 0.5 for c in centers] + areas + [disp_ref[0:1, :]]):
        main = jnp.where(row == r, value, main)
    lane = lax.broadcasted_iota(jnp.int32, (8, LANES), 1)
    coef[...] = jnp.zeros_like(coef)
    coef[0:4, 0:per_dev] = coef_ref[...]
    spread = jnp.take_along_axis(coef[...], lane % per_dev, axis=1, mode="promise_in_bounds")
    per_tile = LANES // per_dev
    spread = jnp.where(lane // per_dev == lax.rem(me, per_tile), spread, 0.0)
    held[me, :, 0:width] = main
    for t in range(width // LANES):
        held[me, t : t + 1, width : width + LANES] = disp_ref[2:3, t * LANES : (t + 1) * LANES]
    held[me, :, width + LANES : width + 2 * LANES] = spread

    def copy(source, device, sem):
        return pltpu.make_async_remote_copy(
            src_ref=held.at[source],
            dst_ref=held.at[source],
            send_sem=send_sem.at[sem],
            recv_sem=recv_sem.at[source],
            device_id={"blk": device},
            device_id_type=pl.DeviceIdType.MESH,
        )

    def to_sibling(step):
        return copy(block_of(step), sibling, step)

    def to_inner(step, j):
        return copy(block_of(step), inner_peer(j), chips + step * inner + j)

    def to_outer(j):
        return copy(me, outer_peer(j), 2 * chips + j)

    def arrived(source):
        copy(source, sibling, 0).wait_recv()

    def pass_on(step):
        arrived(block_of(step))
        to_sibling(step).start()

    def pass_column(step):
        arrived(block_of(step))
        each(1, inner, lambda j: to_inner(step, j).start())
        to_sibling(step).start()

    pl.semaphore_wait(barrier, outer + inner - 1)
    each(1, outer, lambda j: to_outer(j).start())
    each(1, inner, lambda j: to_inner(0, j).start())
    to_sibling(0).start()

    corner = [c[:, 0:targets] for c in corner]
    points, normals = triangles(corner, 3)
    x = [p - 0.5 for p in points]
    near_t[...] = target_features(x)
    sums[...] = jnp.zeros_like(sums)

    def add_blocks(sources):
        left, right = [], []
        for source in sources:
            near, weights = source_features(held[source], width)
            dist_sq = lax.dot_general(
                near, near_t[...], (((0,), (0,)), ((), ())), preferred_element_type=f32
            )
            inv = lax.rsqrt(dist_sq)
            cube = inv * inv * inv
            high = cube.astype(bf16)
            low = (cube - high.astype(f32)).astype(bf16)
            left += [weights, weights]
            right += [high, low]
        sums[...] += jnp.dot(
            jnp.concatenate(left, axis=1), jnp.concatenate(right, axis=0), preferred_element_type=f32
        )

    def add_chip(step):
        own = block_of(step)
        other = own + 1 - 2 * core
        arrived(other)
        add_blocks([own, other])

    add_chip(0)
    each(1, outer, pass_column)
    ahead = min(outer + 1, chips)
    each(outer, ahead, pass_on)

    def pass_and_add(step):
        pass_on(step + ahead - 1)
        add_chip(step)

    each(1, chips - ahead + 1, pass_and_add)
    each(chips - ahead + 1, chips, add_chip)

    total = sums[0:48, :]
    for piece in range(1, PIECES):
        total = total + sums[48 * piece : 48 * piece + 48, :]
    influence = combine(total, x, normals)

    tables = -(-n_dev * per_dev // LANES)
    which = jnp.broadcast_to(frac_ref[...], (8, targets))
    low, high = which % LANES, which // LANES
    picked = jnp.zeros((8, targets), f32)
    for g in range(tables):
        table = jnp.zeros((8, LANES), f32)
        for s in range(g * per_tile, min((g + 1) * per_tile, n_dev)):
            table = table + held[s, :, width + LANES : width + 2 * LANES]
        got = jnp.concatenate(
            [
                jnp.take_along_axis(
                    table, low[:, t * LANES : (t + 1) * LANES], axis=1, mode="promise_in_bounds"
                )
                for t in range(targets // LANES)
            ],
            axis=1,
        )
        picked = jnp.where(high == g, got, picked)
    pressure = picked[0:1]
    for k in range(3):
        pressure = pressure + picked[k + 1 : k + 2] * points[k]
    gain = force_gain / math.sqrt(width * n_dev)
    for m in range(3):
        out_ref[m : m + 1, :] = gain * influence[m] - pressure * normals[m]

    each(1, outer, lambda j: to_outer(j).wait_send())
    each(0, outer, lambda step: each(1, inner, lambda j: to_inner(step, j).wait_send()))
    each(0, chips, lambda step: to_sibling(step).wait_send())


def solution(mesh):
    n_dev = mesh.shape["blk"]

    def local(vertices, source_tri, source_disp, target_tri, fracture_of, pressure_coeffs):
        width, targets = source_tri.shape[1], target_tri.shape[1]
        vmem = pl.BlockSpec(memory_space=pltpu.VMEM)
        return pl.pallas_call(
            functools.partial(kernel, n_dev),
            out_shape=jax.ShapeDtypeStruct((3, targets), f32),
            in_specs=[vmem] * 6,
            out_specs=vmem,
            scratch_shapes=[
                pltpu.VMEM((n_dev, 8, width + 2 * LANES), f32),
                pltpu.VMEM((8, width), jnp.int32),
                pltpu.VMEM((8, LANES), f32),
                pltpu.VMEM((80, targets), bf16),
                pltpu.VMEM((48 * PIECES, targets), f32),
                pltpu.SemaphoreType.DMA((2 * n_dev,)),
                pltpu.SemaphoreType.DMA((n_dev,)),
            ],
            compiler_params=pltpu.CompilerParams(
                collective_id=0, has_side_effects=True, vmem_limit_bytes=48 << 20
            ),
        )(vertices, source_tri, source_disp, target_tri, fracture_of[None, :], pressure_coeffs)

    both = ("groups", "blk")
    wide = P(None, both)
    return jax.shard_map(
        local, mesh=mesh, in_specs=(wide, wide, wide, wide, P(both), wide), out_specs=wide, check_vma=False
    )
```

```python
import functools
import math

import jax
import jax.numpy as jnp
from jax import lax
from jax.experimental import pallas as pl
from jax.experimental.pallas import tpu as pltpu
from jax.sharding import PartitionSpec as P

core_sq = 0.01
force_gain = 40.0
LANES = 128
PIECES = 3
f32 = jnp.float32
bf16 = jnp.bfloat16


def split(value, pieces):
    out = []
    for _ in range(pieces):
        piece = value.astype(bf16).astype(f32)
        out.append(piece)
        value = value - piece
    return out


def lookup(table, index):
    columns = []
    for t in range(index.shape[1] // LANES):
        where = index[:, t * LANES : (t + 1) * LANES]
        low, high = where & (LANES - 1), where >> 7
        got = None
        for c in range(table.shape[1] // LANES):
            part = jnp.broadcast_to(table[:, c * LANES : (c + 1) * LANES], (8, LANES))
            part = jnp.take_along_axis(part, low, axis=1, mode="promise_in_bounds")
            got = part if got is None else jnp.where(high == c, part, got)
        columns.append(got)
    return jnp.concatenate(columns, axis=1)


def triangles(corner, first):
    p0, p1, p2 = ([corner[k][first + c : first + c + 1] for k in range(3)] for c in range(3))
    centers = [(p0[k] + p1[k] + p2[k]) / 3.0 for k in range(3)]
    u = [p1[k] - p0[k] for k in range(3)]
    v = [p2[k] - p0[k] for k in range(3)]
    areas = [0.5 * (u[(k + 1) % 3] * v[(k + 2) % 3] - u[(k + 2) % 3] * v[(k + 1) % 3]) for k in range(3)]
    return centers, areas


def source_features(block, width):
    main = block[:, :width]
    row = lax.broadcasted_iota(jnp.int32, (8, width), 0)
    y = [main[k : k + 1] for k in range(3)]
    a = [main[3 + k : 4 + k] for k in range(3)]
    d = [main[6:7], main[7:8]]
    d.append(
        jnp.concatenate([block[t : t + 1, width : width + LANES] for t in range(width // LANES)], axis=1)
    )
    m1, m2, m3 = split(main, 3)
    q1, q2, q3 = split(main * main, 3)
    ones = jnp.ones((8, width), f32)
    near = jnp.concatenate([m1, m1, m1, m2, m2, m3, q1, q2, q3, ones], axis=0).astype(bf16)
    outer = lambda t: jnp.where(row < 3, t[0], jnp.where(row < 6, t[1], t[2]))
    inner = lambda t: jnp.where(row % 3 == 0, t[0], jnp.where(row % 3 == 1, t[1], t[2]))
    yy = y[0] * y[0] + y[1] * y[1] + y[2] * y[2] + core_sq
    yd = y[0] * d[0] + y[1] * d[1] + y[2] * d[2]
    q = outer(a) * inner(d)
    last = a[2] * d[2]
    last_c = yy * last + y[2] * yd * a[2]
    tiles = [q, y[0] * q, y[1] * q, y[2] * q, yy * q + (yd * outer(y)) * inner(a)]
    tail = jnp.where(row == 0, last, 0.0)
    for k in range(3):
        tail = jnp.where(row == k + 1, y[k] * last, tail)
    tail = jnp.where(row == 4, last_c, tail)
    weights = split(jnp.concatenate(tiles + [tail], axis=0), PIECES)
    return near, jnp.concatenate(weights, axis=0).astype(bf16)


def target_features(x):
    width = x[0].shape[1]
    row = lax.broadcasted_iota(jnp.int32, (8, width), 0)
    coords = jnp.where(row == 0, x[0], jnp.where(row == 1, x[1], jnp.where(row == 2, x[2], 0.0)))
    x1, x2, x3 = split(-2.0 * coords, 3)
    square = x[0] * x[0] + x[1] * x[1] + x[2] * x[2] + core_sq
    s1, s2, s3 = split(square, 3)
    const = jnp.where(row == 0, s1, jnp.where(row == 1, s2, jnp.where(row == 2, s3, 0.0)))
    first3 = jnp.where(row < 3, 1.0, 0.0)
    return jnp.concatenate([x1, x2, x3, x1, x2, x1, first3, first3, first3, const], axis=0).astype(bf16)


def combine(sums, x, n):
    def pick(tile, k, m):
        r = 3 * k + m
        at = 8 * tile + r if r < 8 else 40 + tile
        return sums[at : at + 1]

    first = [[pick(0, k, m) for m in range(3)] for k in range(3)]
    moved = [[[pick(1 + p, k, m) for m in range(3)] for k in range(3)] for p in range(3)]
    const = [[pick(4, k, m) for m in range(3)] for k in range(3)]
    xx = x[0] * x[0] + x[1] * x[1] + x[2] * x[2]
    nx = n[0] * x[0] + n[1] * x[1] + n[2] * x[2]
    rows = []
    for m in range(3):
        total = 0.0
        for k in range(3):
            inside = xx * first[k][m] + const[k][m]
            for p in range(3):
                inside = inside - x[p] * (2.0 * moved[p][k][m] + moved[k][m][p])
            total = total + n[k] * inside
            total = total + nx * (x[k] * first[m][k] - moved[k][m][k])
        rows.append(total)
    return rows


def kernel(
    n_dev, vert_in, stri_in, disp_in, ttri_in, frac_in, coef_in, out_ref,
    vert_ref, stri_ref, disp_ref, ttri_ref, frac_ref, coef_ref,
    held, index, coef, near_t, sums, load_sem, send_sem, recv_sem,
):
    pairs = [
        (vert_in, vert_ref), (stri_in, stri_ref), (ttri_in, ttri_ref),
        (disp_in, disp_ref), (coef_in, coef_ref), (frac_in, frac_ref),
    ]
    loads = [pltpu.make_async_copy(src, dst, load_sem.at[k]) for k, (src, dst) in enumerate(pairs)]
    for load in loads:
        load.start()
    me = lax.axis_index("blk")
    width = stri_ref.shape[1]
    targets = ttri_ref.shape[1]
    per_dev = coef_ref.shape[1]
    chips = n_dev // 2
    inner = 1 << (chips.bit_length() - 1) // 2
    outer = chips // inner
    core = lax.rem(me, 2)
    sibling = me + 1 - 2 * core
    row_at = lax.rem(me // 2, inner)
    column_at = me // (2 * inner)

    def block_of(step):
        o = lax.rem(column_at - lax.rem(step, outer) + outer, outer)
        i = lax.rem(row_at - step // outer + inner, inner)
        return (o * inner + i) * 2 + core

    def outer_peer(step):
        return (lax.rem(column_at + step, outer) * inner + row_at) * 2 + core

    def inner_peer(step):
        return (column_at * inner + lax.rem(row_at + step, inner)) * 2 + core

    barrier = pltpu.get_barrier_semaphore()

    def greet(device):
        pl.semaphore_signal(
            barrier, inc=1, device_id={"blk": device}, device_id_type=pl.DeviceIdType.MESH
        )

    def each(low, high, act):
        def body(step, _):
            act(step)
            return 0

        lax.fori_loop(low, high, body, 0)

    greet(sibling)
    each(1, outer, lambda j: greet(outer_peer(j)))
    each(1, inner, lambda j: greet(inner_peer(j)))

    index[...] = jnp.zeros_like(index)
    for load in loads:
        load.wait()
    index[0:3, :] = stri_ref[...]
    index[3:6, 0:targets] = ttri_ref[...]
    spots = index[...]
    corner = [lookup(vert_ref[k : k + 1, :], spots) for k in range(3)]
    centers, areas = triangles(corner, 0)
    row = lax.broadcasted_iota(jnp.int32, (8, width), 0)
    main = disp_ref[1:2, :]
    for r, value in enumerate([c - 0.5 for c in centers] + areas + [disp_ref[0:1, :]]):
        main = jnp.where(row == r, value, main)
    lane = lax.broadcasted_iota(jnp.int32, (8, LANES), 1)
    coef[...] = jnp.zeros_like(coef)
    coef[0:4, 0:per_dev] = coef_ref[...]
    spread = jnp.take_along_axis(coef[...], lane % per_dev, axis=1, mode="promise_in_bounds")
    per_tile = LANES // per_dev
    spread = jnp.where(lane // per_dev == lax.rem(me, per_tile), spread, 0.0)
    held[me, :, 0:width] = main
    for t in range(width // LANES):
        held[me, t : t + 1, width : width + LANES] = disp_ref[2:3, t * LANES : (t + 1) * LANES]
    held[me, :, width + LANES : width + 2 * LANES] = spread

    def copy(source, device, sem):
        return pltpu.make_async_remote_copy(
            src_ref=held.at[source],
            dst_ref=held.at[source],
            send_sem=send_sem.at[sem],
            recv_sem=recv_sem.at[source],
            device_id={"blk": device},
            device_id_type=pl.DeviceIdType.MESH,
        )

    def to_sibling(step):
        return copy(block_of(step), sibling, step)

    def to_inner(step, j):
        return copy(block_of(step), inner_peer(j), chips + step * inner + j)

    def to_outer(j):
        return copy(me, outer_peer(j), 2 * chips + j)

    def arrived(source):
        copy(source, sibling, 0).wait_recv()

    def pass_on(step):
        arrived(block_of(step))
        to_sibling(step).start()

    def pass_column(step):
        arrived(block_of(step))
        each(1, inner, lambda j: to_inner(step, j).start())
        to_sibling(step).start()

    pl.semaphore_wait(barrier, outer + inner - 1)
    each(1, outer, lambda j: to_outer(j).start())
    each(1, inner, lambda j: to_inner(0, j).start())
    to_sibling(0).start()

    corner = [c[:, 0:targets] for c in corner]
    points, normals = triangles(corner, 3)
    x = [p - 0.5 for p in points]
    near_t[...] = target_features(x)
    sums[...] = jnp.zeros_like(sums)

    def add_blocks(sources):
        left, right = [], []
        for source in sources:
            near, weights = source_features(held[source], width)
            dist_sq = lax.dot_general(
                near, near_t[...], (((0,), (0,)), ((), ())), preferred_element_type=f32
            )
            inv = lax.rsqrt(dist_sq)
            cube = inv * inv * inv
            high = cube.astype(bf16)
            low = (cube - high.astype(f32)).astype(bf16)
            left += [weights, weights]
            right += [high, low]
        sums[...] += jnp.dot(
            jnp.concatenate(left, axis=1), jnp.concatenate(right, axis=0), preferred_element_type=f32
        )

    def add_chip(step):
        own = block_of(step)
        other = own + 1 - 2 * core
        arrived(other)
        add_blocks([own, other])

    add_chip(0)
    each(1, outer, pass_column)
    ahead = min(outer + 1, chips)
    each(outer, ahead, pass_on)

    def pass_and_add(step):
        pass_on(step + ahead - 1)
        add_chip(step)

    each(1, chips - ahead + 1, pass_and_add)
    each(chips - ahead + 1, chips, add_chip)

    total = sums[0:48, :]
    for piece in range(1, PIECES):
        total = total + sums[48 * piece : 48 * piece + 48, :]
    influence = combine(total, x, normals)

    tables = -(-n_dev * per_dev // LANES)
    which = jnp.broadcast_to(frac_ref[...], (8, targets))
    low, high = which & (LANES - 1), which >> 7
    picked = jnp.zeros((8, targets), f32)
    for g in range(tables):
        table = jnp.zeros((8, LANES), f32)
        for s in range(g * per_tile, min((g + 1) * per_tile, n_dev)):
            table = table + held[s, :, width + LANES : width + 2 * LANES]
        got = jnp.concatenate(
            [
                jnp.take_along_axis(
                    table, low[:, t * LANES : (t + 1) * LANES], axis=1, mode="promise_in_bounds"
                )
                for t in range(targets // LANES)
            ],
            axis=1,
        )
        picked = jnp.where(high == g, got, picked)
    pressure = picked[0:1]
    for k in range(3):
        pressure = pressure + picked[k + 1 : k + 2] * points[k]
    gain = force_gain / math.sqrt(width * n_dev)
    for m in range(3):
        out_ref[m : m + 1, :] = gain * influence[m] - pressure * normals[m]

    each(1, outer, lambda j: to_outer(j).wait_send())
    each(0, outer, lambda step: each(1, inner, lambda j: to_inner(step, j).wait_send()))
    each(0, chips, lambda step: to_sibling(step).wait_send())


def solution(mesh):
    n_dev = mesh.shape["blk"]

    def local(vertices, source_tri, source_disp, target_tri, fracture_of, pressure_coeffs):
        width, targets = source_tri.shape[1], target_tri.shape[1]
        vmem = pl.BlockSpec(memory_space=pltpu.VMEM)
        args = (vertices, source_tri, source_disp, target_tri, fracture_of[None, :], pressure_coeffs)
        return pl.pallas_call(
            functools.partial(kernel, n_dev),
            out_shape=jax.ShapeDtypeStruct((3, targets), f32),
            in_specs=[pl.BlockSpec(memory_space=pl.ANY)] * 6,
            out_specs=vmem,
            scratch_shapes=[pltpu.VMEM(a.shape, a.dtype) for a in args]
            + [
                pltpu.VMEM((n_dev, 8, width + 2 * LANES), f32),
                pltpu.VMEM((8, width), jnp.int32),
                pltpu.VMEM((8, LANES), f32),
                pltpu.VMEM((80, targets), bf16),
                pltpu.VMEM((48 * PIECES, targets), f32),
                pltpu.SemaphoreType.DMA((6,)),
                pltpu.SemaphoreType.DMA((2 * n_dev,)),
                pltpu.SemaphoreType.DMA((n_dev,)),
            ],
            compiler_params=pltpu.CompilerParams(
                collective_id=0, has_side_effects=True, vmem_limit_bytes=64 << 20
            ),
        )(*args)

    both = ("groups", "blk")
    wide = P(None, both)
    return jax.shard_map(
        local, mesh=mesh, in_specs=(wide, wide, wide, wide, P(both), wide), out_specs=wide, check_vma=False
    )
```
